128 devices in a mesh: gx: 8 (over x, core), gy: 16 (over z, y).
Axes of the slice: x: 4, y: 4, z: 4, core: 2. Of those that a mesh axis runs over, the one named last changes fastest.
Arguments:
- hidden_in: bfloat16 [1024, 16384], P('gx', 'gy'), may hold values from -6 to 6
- w_query: bfloat16 [16384, 16384], P('gy', 'gx'), may hold values from -0.046875 to 0.046875
- w_key: bfloat16 [16384, 1024], P('gy', 'gx'), may hold values from -0.046875 to 0.046875
- w_value: bfloat16 [16384, 1024], P('gy', 'gx'), may hold values from -0.046875 to 0.046875
- w_output: bfloat16 [16384, 16384], P('gx', 'gy'), may hold values from -0.046875 to 0.046875
- cache_keys: bfloat16 [1024, 448, 1024], P(('gx', 'gy')), may hold values from -210 to 210, as said below
- cache_values: bfloat16 [1024, 448, 1024], P(('gx', 'gy')), may hold values from -6 to 6
- cache_lengths: int32 [1024], P(('gx', 'gy')), may hold values from 2 to 448, as said below
- positions: int32 [1024], P(('gx', 'gy')), may hold values from 448 to 8191
Outputs:
- attended: bfloat16 [1024, 16384], P('gx', 'gy')
- new_keys: bfloat16 [1024, 1024], P(('gx', 'gy'))
- new_values: bfloat16 [1024, 1024], P(('gx', 'gy'))
The draws below stay inside these ranges and needn't reach their ends.
Inputs may be any that keep to these rules, and one draw needn't show every extreme that they name: `cache_lengths`: each sequence has at least two filled slots; some sequence has all 448 slots filled. `cache_keys`: A few slots of a sequence may hold keys of magnitude up to about 205.
All inputs are finite; a program needn't handle non-finite values.
Results may differ from the reference program's by a relative error of at most 0.012.
The reference program's roundings to bfloat16 on the way (of `queries`, `keys_lin`, `rotated_q`, `weights` and `mixed`) count: a program that leaves them out, or rounds other values in their place, can miss the bound.
Values may be sent and summed in bfloat16 or wider, within the bound.
No kernel may reach another device: no remote copies, remote signals or barrier semaphores. Data moves between devices by JAX's collectives and lax.ppermute only.
A program may use at most 128 MiB of HBM per device.

```python
import math
import jax
import jax.numpy as jnp
from jax import lax

D = 16384
HQ = 128
KVH = 8
DH = 128
CACHE = 448
GROUP = 16
B = 1024


def draw_cache_keys(key, part):
    key = jax.random.fold_in(key, 11)
    key_base = jax.random.fold_in(key, 0)
    values = jax.random.truncated_normal(key_base, -6.0, 6.0, (B, CACHE, KVH * DH), jnp.float32)
    return values.astype(jnp.bfloat16)


def draw_cache_lengths(key, part):
    key = jax.random.fold_in(key, 23)
    key_lengths, key_full = jax.random.split(key)
    lengths = jax.random.randint(key_lengths, (B,), 2, CACHE + 1, jnp.int32)
    full_row = jax.random.randint(key_full, (), 0, B, jnp.int32)
    return jnp.where(jnp.arange(B, dtype=jnp.int32) == full_row, CACHE, lengths).astype(jnp.int32)


def touch_ends(array, key, low, top_value):
    longest = array.shape.index(max(array.shape))
    spots = []
    for shift in (0, 1):
        where = [jax.random.randint(jax.random.fold_in(key, axis), (), 0, length) for axis, length in enumerate(array.shape)]
        where[longest] = (where[longest] + shift) % array.shape[longest]
        spots.append(tuple(where))
    return array.at[spots[0]].set(low).at[spots[1]].set(top_value)


def block_scale(own_key, dims, pieces, smallest, high):
    level = 1.0
    for position, parts in pieces:
        heights = jax.random.uniform(jax.random.fold_in(jax.random.fold_in(own_key, 6), position), (parts,), jnp.float32, smallest / len(pieces), high / len(pieces))
        level = level * jnp.repeat(jnp.exp(heights), dims[position] // parts).reshape((-1,) + (1,) * (len(dims) - 1 - position))
    return level


def centred(rng, extent, deviation, limit, pieces=(), kind=jnp.bfloat16):
    entries = deviation * jax.random.normal(rng, extent, jnp.float32)
    if pieces:
        entries = entries * block_scale(rng, extent, pieces, -0.22, 0.18)
    return jnp.clip(entries, -limit, limit).astype(kind)


def setup_inputs(seed: int = 0) -> dict:
    splits = jax.random.split(jax.random.key(seed), 10)
    return {
        "hidden_in": centred(splits[0], (B, D), 1.0, 6.0, ((0, 8), (1, 16))),
        "w_query": centred(splits[1], (D, HQ * DH), D ** -0.5, 0.046875, ((0, 16), (1, 8))),
        "w_key": centred(splits[2], (D, KVH * DH), D ** -0.5, 0.046875, ((0, 16), (1, 8))),
        "w_value": centred(splits[3], (D, KVH * DH), D ** -0.5, 0.046875, ((0, 16), (1, 8))),
        "w_output": centred(splits[4], (HQ * DH, D), (HQ * DH) ** -0.5, 0.046875, ((0, 8), (1, 16))),
        "cache_keys": draw_cache_keys(jax.random.fold_in(splits[9], 71), 0),
        "cache_values": centred(splits[6], (B, CACHE, KVH * DH), 1.0, 6.0, ((0, 128),)),
        "cache_lengths": draw_cache_lengths(jax.random.fold_in(splits[9], 71), 0),
        "positions": touch_ends(jax.random.randint(splits[8], (B,), CACHE, 8192), jax.random.fold_in(splits[8], 1), CACHE, 8191).astype(jnp.int32),
    }


def rope_frequencies():
    index = jnp.arange(DH // 2, dtype=jnp.float32)
    base = jnp.power(jnp.float32(500000.0), -2.0 * index / DH)
    wavelength = 2.0 * math.pi / base
    smooth = (8192.0 / wavelength - 1.0) / 3.0
    middle = (1.0 - smooth) * base / 8.0 + smooth * base
    return jnp.where(wavelength > 8192.0, base / 8.0, jnp.where(wavelength < 2048.0, base, middle))


def rotate(vectors, where_at):
    angle = where_at.astype(jnp.float32)[:, None] * rope_frequencies()[None, :]
    cosine = jnp.cos(angle)[:, None, :]
    sine = jnp.sin(angle)[:, None, :]
    first_half = vectors[..., : DH // 2]
    second_half = vectors[..., DH // 2:]
    return jnp.concatenate([first_half * cosine - second_half * sine, second_half * cosine + first_half * sine], axis=-1)


def attend_one(items):
    query_rot, keys_old, values_old, key_new, value_new, length = items
    query_grouped = query_rot.reshape(KVH, GROUP, DH).astype(jnp.float32)
    keys_three = keys_old.reshape(CACHE, KVH, DH).astype(jnp.float32)
    values_three = values_old.reshape(CACHE, KVH, DH).astype(jnp.float32)
    key_new3 = key_new.reshape(KVH, DH).astype(jnp.float32)
    value_new3 = value_new.reshape(KVH, DH).astype(jnp.float32)
    scale = DH ** -0.5
    scores = jnp.einsum("hgd,lhd->hgl", query_grouped, keys_three) * scale
    keep = jnp.arange(CACHE) < length
    scores = jnp.where(keep[None, None, :], scores, -jnp.inf)
    score_new = jnp.einsum("hgd,hd->hg", query_grouped, key_new3) * scale
    top = jnp.maximum(jnp.max(scores, axis=-1), score_new)
    expo = jnp.exp(scores - top[..., None])
    expo_new = jnp.exp(score_new - top)
    total = jnp.sum(expo, axis=-1) + expo_new
    weights = (expo / total[..., None]).astype(jnp.bfloat16)
    weight_new = (expo_new / total).astype(jnp.bfloat16)
    mixed = jnp.einsum("hgl,lhd->hgd", weights.astype(jnp.float32), values_three)
    mixed = mixed + weight_new.astype(jnp.float32)[..., None] * value_new3[:, None, :]
    return mixed.reshape(HQ * DH).astype(jnp.bfloat16)


def reference(hidden_in, w_query, w_key, w_value, w_output, cache_keys, cache_values, cache_lengths, positions):
    queries = jnp.dot(hidden_in, w_query, preferred_element_type=jnp.float32).astype(jnp.bfloat16)
    keys_lin = jnp.dot(hidden_in, w_key, preferred_element_type=jnp.float32).astype(jnp.bfloat16)
    new_values = jnp.dot(hidden_in, w_value, preferred_element_type=jnp.float32).astype(jnp.bfloat16)
    rotated_q = rotate(queries.astype(jnp.float32).reshape(B, HQ, DH), positions).astype(jnp.bfloat16)
    new_keys = rotate(keys_lin.astype(jnp.float32).reshape(B, KVH, DH), positions).astype(jnp.bfloat16).reshape(B, KVH * DH)
    mixed = lax.map(attend_one, (rotated_q, cache_keys, cache_values, new_keys, new_values, cache_lengths))
    attended = jnp.dot(mixed, w_output, preferred_element_type=jnp.float32).astype(jnp.bfloat16)
    return attended, new_keys, new_values
```

```python
import functools
import math

import jax
import jax.numpy as jnp
from jax import lax
from jax.experimental import pallas as pl
from jax.experimental.pallas import tpu as pltpu
from jax.sharding import PartitionSpec as P

HQ = 128
KVH = 8
DH = 128
CACHE = 448
GROUP = HQ // KVH
AXES = ("gx", "gy")
SIDE = 4
ROWS = 8
LIFT = 32.0


def rope_frequencies():
    index = jnp.arange(DH // 2, dtype=jnp.float32)
    base = jnp.power(jnp.float32(500000.0), -2.0 * index / DH)
    wavelength = 2.0 * math.pi / base
    smooth = (8192.0 / wavelength - 1.0) / 3.0
    middle = (1.0 - smooth) * base / 8.0 + smooth * base
    return jnp.where(wavelength > 8192.0, base / 8.0, jnp.where(wavelength < 2048.0, base, middle))


def shift(value, dx=0, dc=0, dy=0, dz=0):
    pairs = []
    for x in range(SIDE):
        for c in range(2):
            for z in range(SIDE):
                for y in range(SIDE):
                    source = (x * 2 + c) * 16 + z * SIDE + y
                    target = (((x + dx) % SIDE) * 2 + (c ^ dc)) * 16
                    target += ((z + dz) % SIDE) * SIDE + (y + dy) % SIDE
                    pairs.append((source, target))
    return lax.ppermute(value, AXES, pairs)


def order_kernel(place, h_ref, a_ref, b_ref):
    z, y = place[0], place[1]
    for dz in range(SIDE):
        for dy in range(SIDE):
            rows = h_ref[lax.rem(z + dz, SIDE) * SIDE + lax.rem(y + dy, SIDE)]
            a_ref[dy, dz] = rows
            b_ref[dz, dy] = rows


def order_rows(place, hidden):
    width = hidden.shape[1]
    shape = jax.ShapeDtypeStruct((SIDE, SIDE, ROWS, width), hidden.dtype)
    return pl.pallas_call(
        order_kernel,
        out_shape=(shape, shape),
        in_specs=[pl.BlockSpec(memory_space=pltpu.SMEM), pl.BlockSpec(memory_space=pltpu.VMEM)],
        out_specs=(pl.BlockSpec(memory_space=pltpu.VMEM),) * 2,
        cost_estimate=pl.CostEstimate(flops=0, bytes_accessed=3 * 2**18, transcendentals=0),
        name="order_rows",
    )(place, hidden.reshape(SIDE * SIDE, ROWS, width))


def sum_over_plane(near_y, near_z, weights):
    n = len(near_y)
    width = weights.shape[1]
    rows = SIDE * SIDE * n * ROWS
    stacked = jnp.concatenate(
        [jnp.stack(part, axis=2).reshape(rows, -1) for part in (near_y, near_z)], axis=0
    )
    product = jnp.dot(stacked, weights, preferred_element_type=jnp.float32)
    product = (product * LIFT).astype(jnp.float16)
    parts = [product[:rows], product[rows:]]
    for first in (True, False):
        shape = (SIDE, rows // SIDE, width) if first else (SIDE, n * ROWS, width)
        parts = [part.reshape(shape) for part in parts]
        came = [[], []]
        for step in (1, 3, 2):
            for which in range(2):
                along = "dy" if (which == 0) == first else "dz"
                came[which].append(shift(parts[which][step].astype(jnp.float16), **{along: step}))
        parts = [
            functools.reduce(
                jnp.add,
                [part[0].astype(jnp.float32)] + [item.astype(jnp.float32) for item in items],
            )
            for part, items in zip(parts, came)
        ]
    return [
        (part * (1.0 / LIFT)).astype(jnp.bfloat16).reshape(n, ROWS, width) for part in parts
    ]


def attention_kernel(
    head, length, q_ref, cos_ref, sin_ref, k_ref, v_ref, o_ref, nk_ref, nv_ref, queries, results
):
    cosine = cos_ref[...]
    sine = sin_ref[...]

    def rotated(columns):
        u = q_ref[0, :, columns].astype(jnp.float32)
        return (u * cosine + pltpu.roll(u, DH // 2, 1) * sine).astype(jnp.bfloat16)

    for h in range(GROUP):
        queries[pl.ds(h, ROWS, stride=GROUP), :] = rotated(
            slice(h * DH, (h + 1) * DH)
        ).astype(jnp.float32)
    key_new = rotated(slice(GROUP * DH, (GROUP + 1) * DH))
    nk_ref[...] = key_new
    value_new = q_ref[0, :, (GROUP + 1) * DH :]
    nv_ref[...] = value_new
    key_new = key_new.astype(jnp.float32)
    value_new = value_new.astype(jnp.float32)
    scale = DH ** (-0.5)
    slot = lax.broadcasted_iota(jnp.int32, (GROUP, CACHE), 1)
    for s in range(ROWS):
        q = queries[s * GROUP : (s + 1) * GROUP, :]
        scores = lax.dot_general(
            q.astype(jnp.bfloat16),
            k_ref[s],
            (((1,), (1,)), ((), ())),
            preferred_element_type=jnp.float32,
        )
        scores = jnp.where(slot < length[s], scores * scale, -jnp.inf)
        score_new = jnp.sum(q * key_new[s : s + 1], axis=1, keepdims=True) * scale
        top = jnp.maximum(jnp.max(scores, axis=1, keepdims=True), score_new)
        expo = jnp.exp(scores - top)
        expo_new = jnp.exp(score_new - top)
        total = jnp.sum(expo, axis=1, keepdims=True) + expo_new
        weights = (expo / total).astype(jnp.bfloat16)
        weight_new = (expo_new / total).astype(jnp.bfloat16).astype(jnp.float32)
        mixed = jnp.dot(weights, v_ref[s], preferred_element_type=jnp.float32)
        results[s * GROUP : (s + 1) * GROUP, :] = mixed + weight_new * value_new[s : s + 1]
    for h in range(GROUP):
        o_ref[0, :, h * DH : (h + 1) * DH] = results[pl.ds(h, ROWS, stride=GROUP), :].astype(
            jnp.bfloat16
        )


def attention(heads, lengths, packed, cosine, sine, cache_keys, cache_values):
    width = packed.shape[2]
    cache = pl.BlockSpec((ROWS, CACHE, DH), lambda r, head, length: (0, 0, head[r]))
    whole = pl.BlockSpec((ROWS, DH), lambda r, head, length: (0, 0))
    column = pl.BlockSpec((ROWS, DH), lambda r, head, length: (0, head[r]))
    new = jax.ShapeDtypeStruct((ROWS, KVH * DH), jnp.bfloat16)
    return pl.pallas_call(
        attention_kernel,
        out_shape=(jax.ShapeDtypeStruct((KVH, ROWS, GROUP * DH), jnp.bfloat16), new, new),
        grid_spec=pltpu.PrefetchScalarGridSpec(
            num_scalar_prefetch=2,
            grid=(KVH,),
            in_specs=[
                pl.BlockSpec((1, ROWS, width), lambda r, head, length: (r, 0, 0)),
                whole,
                whole,
                cache,
                cache,
            ],
            out_specs=(
                pl.BlockSpec((1, ROWS, GROUP * DH), lambda r, head, length: (r, 0, 0)),
                column,
                column,
            ),
            scratch_shapes=[
                pltpu.VMEM((ROWS * GROUP, DH), jnp.float32),
                pltpu.VMEM((ROWS * GROUP, DH), jnp.float32),
            ],
        ),
        compiler_params=pltpu.CompilerParams(vmem_limit_bytes=24 * 2**20),
        cost_estimate=pl.CostEstimate(
            flops=4 * ROWS * HQ * CACHE * DH,
            bytes_accessed=4 * ROWS * CACHE * KVH * DH,
            transcendentals=ROWS * HQ * CACHE,
        ),
        name="attention",
    )(heads, lengths, packed, cosine, sine, cache_keys, cache_values)


def final_kernel(place, *refs):
    pieces, out_ref = refs[:-1], refs[-1]
    z, y = place[0], place[1]
    at = {0: (0, 0), 1: (1, 0), 3: (1, 1), 2: (2, 0)}
    for dz in range(SIDE):
        for dy in range(SIDE):
            piece_z, in_z = at[dz]
            piece_y, in_y = at[dy]
            own, two = pieces[4 * piece_z : 4 * piece_z + 2]
            one, three = pieces[4 * piece_y + 2 : 4 * piece_y + 4]
            total = own[in_z, dy] + two[in_z, dy].astype(jnp.float32)
            total = total + one[in_y, dz].astype(jnp.float32)
            total = total + three[in_y, dz].astype(jnp.float32)
            where = lax.rem(z - dz + SIDE, SIDE) * SIDE + lax.rem(y - dy + SIDE, SIDE)
            out_ref[where] = total.astype(jnp.bfloat16)


def add_up(place, pieces):
    width = pieces[0].shape[-1]
    return pl.pallas_call(
        final_kernel,
        out_shape=jax.ShapeDtypeStruct((SIDE * SIDE, ROWS, width), jnp.bfloat16),
        in_specs=[pl.BlockSpec(memory_space=pltpu.SMEM)]
        + [pl.BlockSpec(memory_space=pltpu.VMEM)] * len(pieces),
        out_specs=pl.BlockSpec(memory_space=pltpu.VMEM),
        cost_estimate=pl.CostEstimate(flops=2**19, bytes_accessed=2**21, transcendentals=0),
        name="add_up",
    )(place, *pieces)


def project(near_y, near_z, w_output):
    count = len(near_y)
    rows = jnp.concatenate([item.reshape(-1, item.shape[-1]) for item in near_y + near_z], axis=0)
    terms = jnp.dot(rows, w_output, preferred_element_type=jnp.float32)
    terms = terms.reshape(2 * count, SIDE, 2, 2, ROWS, -1)
    other = shift(terms[:, :, 1].astype(jnp.bfloat16), dc=1)
    terms = terms[:, :, 0] + other.astype(jnp.float32)
    own = terms[:count, :, 0]
    two = shift(terms[:count, :, 1].astype(jnp.bfloat16), dx=2)
    one = shift(terms[count:, :, 0].astype(jnp.bfloat16), dx=-1)
    three = shift(terms[count:, :, 1].astype(jnp.bfloat16), dx=1)
    return [own, two, one, three]


def on_device(
    hidden_in, w_query, w_key, w_value, w_output, cache_keys, cache_values, cache_lengths, positions
):
    gx = lax.axis_index("gx")
    gy = lax.axis_index("gy")
    place = jnp.stack([gy // SIDE, gy % SIDE]).astype(jnp.int32)
    x, core = gx // 2, gx % 2

    own_a, own_b = order_rows(place, hidden_in)
    pair_b = shift(own_b, dc=1)
    from_1 = shift(own_a, dx=1)
    from_3 = shift(own_b, dx=3)
    from_2 = shift(own_a, dx=2)
    pair_1 = shift(from_1, dc=1)
    pair_3 = shift(from_3, dc=1)
    pair_2 = shift(from_2.transpose(1, 0, 2, 3), dc=1)
    weights = jnp.concatenate([w_query, w_key, w_value], axis=1)

    summed = {}
    near_y, near_z = sum_over_plane([own_a], [pair_b], weights)
    summed[0, 0], summed[0, 1] = near_y[0], near_z[0]
    near_y, near_z = sum_over_plane([from_1, pair_1], [from_3, pair_3], weights)
    summed[1, 0], summed[1, 1] = near_y[0], near_y[1]
    summed[3, 0], summed[3, 1] = near_z[0], near_z[1]
    near_y, near_z = sum_over_plane([from_2], [pair_2], weights)
    summed[2, 0], summed[2, 1] = near_y[0], near_z[0]

    order = [(dx, dc) for dx in range(SIDE) for dc in range(2)]
    packed = jnp.stack(
        [
            shift(summed[dx, dc], dx=-dx, dc=dc) if (dx, dc) != (0, 0) else summed[dx, dc]
            for dx, dc in order
        ]
    )
    heads = jnp.stack([((x + dx) % SIDE) * 2 + (core + dc) % 2 for dx, dc in order])
    angle = positions.astype(jnp.float32)[:, None] * rope_frequencies()[None, :]
    cosine, sine = jnp.cos(angle), jnp.sin(angle)
    mixed, new_keys, new_values = attention(
        heads.astype(jnp.int32),
        cache_lengths,
        packed,
        jnp.concatenate([cosine, cosine], axis=1),
        jnp.concatenate([-sine, sine], axis=1),
        cache_keys,
        cache_values,
    )

    returned = {
        (dx, dc): shift(mixed[i], dx=dx, dc=dc) if (dx, dc) != (0, 0) else mixed[i]
        for i, (dx, dc) in enumerate(order)
    }
    half_a = jnp.stack([returned[dx, dc] for dc in range(2) for dx in (0, 2)])
    half_b = jnp.stack([returned[dx, dc] for dc in range(2) for dx in (1, 3)])
    row_a = {0: half_a}
    row_b = {0: half_b}
    for step in (1, 3, 2):
        row_a[step] = shift(half_a, dy=step)
        row_b[step] = shift(half_b, dz=step)
    row_a = jnp.stack([row_a[step] for step in range(SIDE)])
    row_b = jnp.stack([row_b[step] for step in range(SIDE)])
    all_a = {0: row_a}
    all_b = {0: row_b}
    for step in (1, 3, 2):
        all_a[step] = shift(row_a, dz=step)
        all_b[step] = shift(row_b, dy=step)
    pieces = []
    for steps in ((0,), (1, 3), (2,)):
        pieces += project([all_a[step] for step in steps], [all_b[step] for step in steps], w_output)
    attended = add_up(place, pieces)
    return (attended.reshape(hidden_in.shape), new_keys, new_values)


def solution(mesh):
    placed = (
        P("gx", "gy"),
        P("gy", "gx"),
        P("gy", "gx"),
        P("gy", "gx"),
        P("gx", "gy"),
        P(("gx", "gy"), None, None),
        P(("gx", "gy"), None, None),
        P(("gx", "gy")),
        P(("gx", "gy")),
    )
    return jax.shard_map(
        on_device,
        mesh=mesh,
        in_specs=placed,
        out_specs=(P("gx", "gy"), P(("gx", "gy"), None), P(("gx", "gy"), None)),
        check_vma=False,
    )
```

```python
import functools
import math

import jax
import jax.numpy as jnp
from jax import lax
from jax.experimental import pallas as pl
from jax.experimental.pallas import tpu as pltpu
from jax.sharding import PartitionSpec as P

HQ = 128
KVH = 8
DH = 128
CACHE = 448
GROUP = HQ // KVH
AXES = ("gx", "gy")
SIDE = 4
ROWS = 8
LIFT = 32.0
PIECES = ((0,), (1, 3), (2,))
FOUND = {step: (p, i) for p, piece in enumerate(PIECES) for i, step in enumerate(piece)}


def rope_frequencies():
    index = jnp.arange(DH // 2, dtype=jnp.float32)
    base = jnp.power(jnp.float32(500000.0), -2.0 * index / DH)
    wavelength = 2.0 * math.pi / base
    smooth = (8192.0 / wavelength - 1.0) / 3.0
    middle = (1.0 - smooth) * base / 8.0 + smooth * base
    return jnp.where(wavelength > 8192.0, base / 8.0, jnp.where(wavelength < 2048.0, base, middle))


def permute(value, move):
    pairs = []
    for x in range(SIDE):
        for c in range(2):
            for z in range(SIDE):
                for y in range(SIDE):
                    tx, tc, tz, ty = move(x, c, z, y)
                    target = ((tx % SIDE) * 2 + tc) * SIDE + tz % SIDE
                    source = (x * 2 + c) * SIDE + z
                    pairs.append((source * SIDE + y, target * SIDE + ty % SIDE))
    return lax.ppermute(value, AXES, pairs)


def to_pair(value):
    return permute(value, lambda x, c, z, y: (x, 1 - c, z, y))


def along_x(value, step):
    return permute(value, lambda x, c, z, y: (x + step, c, z, y))


def along_first(value, step):
    return permute(value, lambda x, c, z, y: (x, c, z + step * c, y + step * (1 - c)))


def along_second(value, step):
    return permute(value, lambda x, c, z, y: (x, c, z + step * (1 - c), y + step * c))


def group_at(place, first, second, sign):
    z, y, core = place[0], place[1], place[2]
    dz = jnp.where(core == 0, second, first)
    dy = jnp.where(core == 0, first, second)
    return lax.rem(z + sign * dz + SIDE, SIDE) * SIDE + lax.rem(y + sign * dy + SIDE, SIDE)


def order_kernel(place, h_ref, out_ref):
    for first in range(SIDE):
        for second in range(SIDE):
            out_ref[first, second] = h_ref[group_at(place, first, second, 1)]


def order_rows(place, hidden):
    width = hidden.shape[1]
    return pl.pallas_call(
        order_kernel,
        out_shape=jax.ShapeDtypeStruct((SIDE, SIDE, ROWS, width), hidden.dtype),
        in_specs=[pl.BlockSpec(memory_space=pltpu.SMEM), pl.BlockSpec(memory_space=pltpu.VMEM)],
        out_specs=pl.BlockSpec(memory_space=pltpu.VMEM),
        cost_estimate=pl.CostEstimate(flops=0, bytes_accessed=2**19, transcendentals=0),
        name="order_rows",
    )(place, hidden.reshape(SIDE * SIDE, ROWS, width))


def total_of(first, others):
    return functools.reduce(
        jnp.add, [first.astype(jnp.float32)] + [item.astype(jnp.float32) for item in others]
    )


def sum_over_plane(groups, weights):
    width = weights.shape[1]
    rows = jnp.stack(groups, axis=2)
    rows = rows.reshape(SIDE, SIDE * len(groups) * ROWS, rows.shape[-1])

    def term(step):
        return jnp.dot(rows[step], weights, preferred_element_type=jnp.float32) * LIFT

    came = [along_first(term(step).astype(jnp.float16), step) for step in (1, 3, 2)]
    kept = total_of(term(0), came).reshape(SIDE, len(groups) * ROWS, width)
    came = [along_second(kept[step].astype(jnp.float16), step) for step in (2, 1, 3)]
    kept = total_of(kept[0], came) * (1.0 / LIFT)
    return kept.astype(jnp.bfloat16).reshape(len(groups), ROWS, width)


def attention_kernel(
    head, length, q_ref, cos_ref, sin_ref, k_ref, v_ref, o_ref, nk_ref, nv_ref, queries, results
):
    cosine = cos_ref[...]
    sine = sin_ref[...]

    def rotated(columns):
        u = q_ref[0, :, columns].astype(jnp.float32)
        return (u * cosine + pltpu.roll(u, DH // 2, 1) * sine).astype(jnp.bfloat16)

    for h in range(GROUP):
        queries[pl.ds(h, ROWS, stride=GROUP), :] = rotated(
            slice(h * DH, (h + 1) * DH)
        ).astype(jnp.float32)
    key_new = rotated(slice(GROUP * DH, (GROUP + 1) * DH))
    nk_ref[...] = key_new
    value_new = q_ref[0, :, (GROUP + 1) * DH :]
    nv_ref[...] = value_new
    key_new = key_new.astype(jnp.float32)
    value_new = value_new.astype(jnp.float32)
    scale = DH ** (-0.5)
    slot = lax.broadcasted_iota(jnp.int32, (GROUP, CACHE), 1)
    for s in range(ROWS):
        q = queries[s * GROUP : (s + 1) * GROUP, :]
        scores = lax.dot_general(
            q.astype(jnp.bfloat16),
            k_ref[s],
            (((1,), (1,)), ((), ())),
            preferred_element_type=jnp.float32,
        )
        scores = jnp.where(slot < length[s], scores * scale, -jnp.inf)
        score_new = jnp.sum(q * key_new[s : s + 1], axis=1, keepdims=True) * scale
        top = jnp.maximum(jnp.max(scores, axis=1, keepdims=True), score_new)
        expo = jnp.exp(scores - top)
        expo_new = jnp.exp(score_new - top)
        total = jnp.sum(expo, axis=1, keepdims=True) + expo_new
        weights = (expo / total).astype(jnp.bfloat16)
        weight_new = (expo_new / total).astype(jnp.bfloat16).astype(jnp.float32)
        mixed = jnp.dot(weights, v_ref[s], preferred_element_type=jnp.float32)
        results[s * GROUP : (s + 1) * GROUP, :] = mixed + weight_new * value_new[s : s + 1]
    for h in range(GROUP):
        o_ref[0, :, h * DH : (h + 1) * DH] = results[pl.ds(h, ROWS, stride=GROUP), :].astype(
            jnp.bfloat16
        )


def attention(heads, lengths, packed, cosine, sine, cache_keys, cache_values):
    width = packed.shape[2] // 2
    cache = pl.BlockSpec((ROWS, CACHE, DH), lambda r, head, length: (0, 0, head[r]))
    whole = pl.BlockSpec((ROWS, DH), lambda r, head, length: (0, 0))
    column = pl.BlockSpec((ROWS, DH), lambda r, head, length: (0, head[r]))
    new = jax.ShapeDtypeStruct((ROWS, KVH * DH), jnp.bfloat16)
    half = (KVH // 2, ROWS, 2 * GROUP * DH)
    return pl.pallas_call(
        attention_kernel,
        out_shape=(jax.ShapeDtypeStruct(half, jnp.bfloat16), new, new),
        grid_spec=pltpu.PrefetchScalarGridSpec(
            num_scalar_prefetch=2,
            grid=(KVH,),
            in_specs=[
                pl.BlockSpec((1, ROWS, width), lambda r, head, length: (r // 2, 0, r % 2)),
                whole,
                whole,
                cache,
                cache,
            ],
            out_specs=(
                pl.BlockSpec((1, ROWS, GROUP * DH), lambda r, head, length: (r // 2, 0, r % 2)),
                column,
                column,
            ),
            scratch_shapes=[
                pltpu.VMEM((ROWS * GROUP, DH), jnp.float32),
                pltpu.VMEM((ROWS * GROUP, DH), jnp.float32),
            ],
        ),
        compiler_params=pltpu.CompilerParams(vmem_limit_bytes=24 * 2**20),
        cost_estimate=pl.CostEstimate(
            flops=4 * ROWS * HQ * CACHE * DH,
            bytes_accessed=4 * ROWS * CACHE * KVH * DH,
            transcendentals=ROWS * HQ * CACHE,
        ),
        name="attention",
    )(heads, lengths, packed, cosine, sine, cache_keys, cache_values)


def final_kernel(place, *refs):
    terms, out_ref = refs[:-1], refs[-1]
    for second in range(SIDE):
        piece, inside = FOUND[second]
        for first in range(SIDE):
            total = terms[4 * piece][inside, first]
            for term in terms[4 * piece + 1 : 4 * piece + 4]:
                total = total + term[inside, first]
            out_ref[group_at(place, first, second, -1)] = total.astype(jnp.bfloat16)


def add_up(place, terms):
    width = terms[0].shape[-1]
    return pl.pallas_call(
        final_kernel,
        out_shape=jax.ShapeDtypeStruct((SIDE * SIDE, ROWS, width), jnp.bfloat16),
        in_specs=[pl.BlockSpec(memory_space=pltpu.SMEM)]
        + [pl.BlockSpec(memory_space=pltpu.VMEM)] * len(terms),
        out_specs=pl.BlockSpec(memory_space=pltpu.VMEM),
        cost_estimate=pl.CostEstimate(flops=2**19, bytes_accessed=2**21, transcendentals=0),
        name="add_up",
    )(place, *terms)


def project(parts, w_output):
    terms = []
    for part in parts:
        term = jnp.dot(part.reshape(-1, part.shape[-1]), w_output, preferred_element_type=jnp.float32)
        terms.append(term.reshape(SIDE, SIDE, ROWS, -1))
    sent = [jnp.stack([term[:, dx] for term in terms]) for dx in range(SIDE)]
    return [sent[0]] + [along_x(sent[dx], -dx) for dx in (2, 1, 3)]


def on_device(
    hidden_in, w_query, w_key, w_value, w_output, cache_keys, cache_values, cache_lengths, positions
):
    gx = lax.axis_index("gx")
    gy = lax.axis_index("gy")
    x, core = gx // 2, gx % 2
    place = jnp.stack([gy // SIDE, gy % SIDE, core]).astype(jnp.int32)

    own = order_rows(place, hidden_in)
    groups = {0: own}
    for step in (2, 1, 3):
        groups[step] = along_x(own, step)
    w_both = jnp.concatenate([w_key, w_value], axis=1)
    w_both = jnp.concatenate([w_query, w_both, to_pair(w_query), to_pair(w_both)], axis=1)
    w_back = jnp.concatenate([w_output, to_pair(w_output)], axis=0)
    summed = sum_over_plane([groups[dx] for dx in range(SIDE)], w_both)

    packed = [along_x(summed[dx], -dx) if dx else summed[dx] for dx in range(SIDE)]
    heads = [((x + dx) % SIDE) * 2 + (core + dc) % 2 for dx in range(SIDE) for dc in range(2)]
    angle = positions.astype(jnp.float32)[:, None] * rope_frequencies()[None, :]
    cosine, sine = jnp.cos(angle), jnp.sin(angle)
    mixed, new_keys, new_values = attention(
        jnp.stack(heads).astype(jnp.int32),
        cache_lengths,
        jnp.stack(packed),
        jnp.concatenate([cosine, cosine], axis=1),
        jnp.concatenate([-sine, sine], axis=1),
        cache_keys,
        cache_values,
    )

    rows = jnp.stack([along_x(mixed[dx], dx) if dx else mixed[dx] for dx in range(SIDE)])
    near = {0: rows}
    for step in (2, 1, 3):
        near[step] = along_first(rows, step)
    rows = jnp.stack([near[step] for step in range(SIDE)])
    far = {0: rows}
    for step in (1, 3, 2):
        far[step] = along_second(rows, step)
    terms = []
    for piece in PIECES:
        terms += project([far[step] for step in piece], w_back)
    attended = add_up(place, terms)
    return (attended.reshape(hidden_in.shape), new_keys, new_values)


def solution(mesh):
    placed = (
        P("gx", "gy"),
        P("gy", "gx"),
        P("gy", "gx"),
        P("gy", "gx"),
        P("gx", "gy"),
        P(("gx", "gy"), None, None),
        P(("gx", "gy"), None, None),
        P(("gx", "gy")),
        P(("gx", "gy")),
    )
    return jax.shard_map(
        on_device,
        mesh=mesh,
        in_specs=placed,
        out_specs=(P("gx", "gy"), P(("gx", "gy"), None), P(("gx", "gy"), None)),
        check_vma=False,
    )
```

```python
import functools
import math

import jax
import jax.numpy as jnp
from jax import lax
from jax.experimental import pallas as pl
from jax.experimental.pallas import tpu as pltpu
from jax.sharding import PartitionSpec as P

HQ = 128
KVH = 8
DH = 128
CACHE = 448
GROUP = HQ // KVH
AXES = ("gx", "gy")
SIDE = 4
ROWS = 8
LIFT = 32.0
PIECES = ((((0, 1, 2, 3),), (1, 3)), (((0, 1, 3), (2,)), (0, 2)))


def rope_frequencies():
    index = jnp.arange(DH // 2, dtype=jnp.float32)
    base = jnp.power(jnp.float32(500000.0), -2.0 * index / DH)
    wavelength = 2.0 * math.pi / base
    smooth = (8192.0 / wavelength - 1.0) / 3.0
    middle = (1.0 - smooth) * base / 8.0 + smooth * base
    return jnp.where(wavelength > 8192.0, base / 8.0, jnp.where(wavelength < 2048.0, base, middle))


def permute(value, move):
    pairs = []
    for x in range(SIDE):
        for c in range(2):
            for z in range(SIDE):
                for y in range(SIDE):
                    tx, tc, tz, ty = move(x, c, z, y)
                    target = ((tx % SIDE) * 2 + tc) * SIDE + tz % SIDE
                    source = (x * 2 + c) * SIDE + z
                    pairs.append((source * SIDE + y, target * SIDE + ty % SIDE))
    return lax.ppermute(value, AXES, pairs)


def to_pair(value):
    return permute(value, lambda x, c, z, y: (x, 1 - c, z, y))


def along_x(value, step):
    return permute(value, lambda x, c, z, y: (x + step, c, z, y))


def along_first(value, step):
    return permute(value, lambda x, c, z, y: (x, c, z + step * c, y + step * (1 - c)))


def along_second(value, step):
    return permute(value, lambda x, c, z, y: (x, c, z + step * (1 - c), y + step * c))


def group_at(place, first, second, sign):
    z, y, core = place[0], place[1], place[2]
    dz = jnp.where(core == 0, second, first)
    dy = jnp.where(core == 0, first, second)
    return lax.rem(z + sign * dz + SIDE, SIDE) * SIDE + lax.rem(y + sign * dy + SIDE, SIDE)


def order_kernel(place, h_ref, out_ref):
    for first in range(SIDE):
        for second in range(SIDE):
            out_ref[first, second] = h_ref[group_at(place, first, second, 1)]


def order_rows(place, hidden):
    width = hidden.shape[1]
    return pl.pallas_call(
        order_kernel,
        out_shape=jax.ShapeDtypeStruct((SIDE, SIDE, ROWS, width), hidden.dtype),
        in_specs=[pl.BlockSpec(memory_space=pltpu.SMEM), pl.BlockSpec(memory_space=pltpu.VMEM)],
        out_specs=pl.BlockSpec(memory_space=pltpu.VMEM),
        cost_estimate=pl.CostEstimate(flops=0, bytes_accessed=2**19, transcendentals=0),
        name="order_rows",
    )(place, hidden.reshape(SIDE * SIDE, ROWS, width))


def total_of(first, others):
    return functools.reduce(
        jnp.add, [first.astype(jnp.float32)] + [item.astype(jnp.float32) for item in others]
    )


def after(value, *others):
    return lax.optimization_barrier((value, *others))[0]


def sum_over_plane(groups, weights, earlier):
    width = weights.shape[1]
    rows = jnp.stack(groups, axis=2)
    terms = jnp.dot(
        rows.reshape(-1, rows.shape[-1]), weights, preferred_element_type=jnp.float32
    )
    terms = (terms * LIFT).astype(jnp.float16).reshape(SIDE, SIDE * len(groups) * ROWS, width)
    came = {}
    for step in (1, 3, 2):
        message = after(terms[step], earlier[step]) if earlier else terms[step]
        came[step] = along_first(message, step)
    kept = total_of(terms[0], came.values()).reshape(SIDE, len(groups) * ROWS, width)
    last = [along_second(kept[step].astype(jnp.float16), step) for step in (2, 1, 3)]
    kept = total_of(kept[0], last) * (1.0 / LIFT)
    return kept.astype(jnp.bfloat16).reshape(len(groups), ROWS, width), came


def attention_kernel(
    place,
    q_ref,
    cos_ref,
    sin_ref,
    mask_ref,
    k_ref,
    v_ref,
    _,
    __,
    o_ref,
    nk_ref,
    nv_ref,
    queries,
    results,
):
    cosine = cos_ref[...]
    sine = sin_ref[...]
    scale = DH ** (-0.5)
    for pair in range(2):
        base = pair * (GROUP + 2) * DH

        def column(h):
            return q_ref[0, :, base + h * DH : base + (h + 1) * DH]

        def rotated(h):
            u = column(h).astype(jnp.float32)
            return (u * cosine + pltpu.roll(u, DH // 2, 1) * sine).astype(jnp.bfloat16)

        head = pl.ds(pl.multiple_of((place[0] + pair) % 2 * DH, DH), DH)
        for h in range(GROUP):
            queries[pair, pl.ds(h, ROWS, stride=GROUP), :] = rotated(h).astype(jnp.float32)
        key_new = rotated(GROUP)
        value_new = column(GROUP + 1)
        nk_ref[:, head] = key_new
        nv_ref[:, head] = value_new
        key_new = key_new.astype(jnp.float32)
        value_new = value_new.astype(jnp.float32)
        q = queries[pair].reshape(ROWS, GROUP, DH)
        scores = lax.dot_general(
            q.astype(jnp.bfloat16),
            k_ref[:, :, head],
            (((2,), (2,)), ((0,), (0,))),
            preferred_element_type=jnp.float32,
        )
        scores = scores * scale + mask_ref[...]
        score_new = jnp.sum(q * key_new[:, None, :], axis=2, keepdims=True) * scale
        top = jnp.maximum(jnp.max(scores, axis=2, keepdims=True), score_new)
        expo = jnp.exp(scores - top)
        expo_new = jnp.exp(score_new - top)
        share = 1.0 / (jnp.sum(expo, axis=2, keepdims=True) + expo_new)
        weights = (expo * share).astype(jnp.bfloat16)
        weight_new = (expo_new * share).astype(jnp.bfloat16).astype(jnp.float32)
        result = lax.dot_general(
            weights,
            v_ref[:, :, head],
            (((2,), (1,)), ((0,), (0,))),
            preferred_element_type=jnp.float32,
        )
        result = result + weight_new * value_new[:, None, :]
        results[pair] = result.reshape(ROWS * GROUP, DH)
        for h in range(GROUP):
            where = (pair * GROUP + h) * DH
            o_ref[0, :, where : where + DH] = results[
                pair, pl.ds(h, ROWS, stride=GROUP), :
            ].astype(jnp.bfloat16)


def attention(place, packed, cosine, sine, mask, cache_keys, cache_values, keys, values):
    steps, _, width = packed.shape
    chip = KVH // SIDE * DH
    cache = pl.BlockSpec((ROWS, CACHE, chip), lambda r, place: (0, 0, place[1 + r]))
    whole = pl.BlockSpec((ROWS, DH), lambda r, place: (0, 0))
    column = pl.BlockSpec((ROWS, chip), lambda r, place: (0, place[1 + r]))
    new = jax.ShapeDtypeStruct((ROWS, KVH * DH), jnp.bfloat16)
    return pl.pallas_call(
        attention_kernel,
        out_shape=(jax.ShapeDtypeStruct((steps, ROWS, chip * GROUP), jnp.bfloat16), new, new),
        grid_spec=pltpu.PrefetchScalarGridSpec(
            num_scalar_prefetch=1,
            grid=(steps,),
            in_specs=[
                pl.BlockSpec((1, ROWS, width), lambda r, place: (r, 0, 0)),
                whole,
                whole,
                pl.BlockSpec((ROWS, GROUP, CACHE), lambda r, place: (0, 0, 0)),
                cache,
                cache,
                pl.BlockSpec(memory_space=pl.ANY),
                pl.BlockSpec(memory_space=pl.ANY),
            ],
            out_specs=(
                pl.BlockSpec((1, ROWS, chip * GROUP), lambda r, place: (r, 0, 0)),
                column,
                column,
            ),
            scratch_shapes=[pltpu.VMEM((2, ROWS * GROUP, DH), jnp.float32)] * 2,
        ),
        input_output_aliases={7: 1, 8: 2},
        compiler_params=pltpu.CompilerParams(vmem_limit_bytes=32 * 2**20),
        cost_estimate=pl.CostEstimate(
            flops=4 * ROWS * HQ * CACHE * DH * steps // SIDE,
            bytes_accessed=4 * ROWS * CACHE * KVH * DH * steps // SIDE,
            transcendentals=ROWS * HQ * CACHE * steps // SIDE,
        ),
        name="attention",
    )(place, packed, cosine, sine, mask, cache_keys, cache_values, keys, values)


def final_kernel(place, *refs):
    terms, out_ref = refs[:-1], refs[-1]
    for second in range(SIDE):
        for first in range(SIDE):
            total = 0.0
            at = 0
            for pieces, group in PIECES:
                for piece in pieces:
                    if second in piece:
                        for term in terms[at : at + len(group)]:
                            total = total + term[piece.index(second), first]
                    at += len(group)
            out_ref[group_at(place, first, second, -1)] = total.astype(jnp.bfloat16)


def add_up(place, terms):
    width = terms[0].shape[-1]
    return pl.pallas_call(
        final_kernel,
        out_shape=jax.ShapeDtypeStruct((SIDE * SIDE, ROWS, width), jnp.bfloat16),
        in_specs=[pl.BlockSpec(memory_space=pltpu.SMEM)]
        + [pl.BlockSpec(memory_space=pltpu.VMEM)] * len(terms),
        out_specs=pl.BlockSpec(memory_space=pltpu.VMEM),
        cost_estimate=pl.CostEstimate(flops=2**19, bytes_accessed=2**21, transcendentals=0),
        name="add_up",
    )(place, *terms)


def project(parts, group, w_output):
    rows = jnp.concatenate([part.reshape(-1, part.shape[-1]) for part in parts], axis=0)
    terms = jnp.dot(rows, w_output, preferred_element_type=jnp.float32)
    terms = terms.reshape(len(parts), SIDE, len(group), ROWS, -1)
    return [along_x(terms[:, :, i], -dx) if dx else terms[:, :, i] for i, dx in enumerate(group)]


def on_device(
    hidden_in, w_query, w_key, w_value, w_output, cache_keys, cache_values, cache_lengths, positions
):
    gx = lax.axis_index("gx")
    gy = lax.axis_index("gy")
    x, core = gx // 2, gx % 2
    place = jnp.stack([gy // SIDE, gy % SIDE, core]).astype(jnp.int32)

    own = order_rows(place, hidden_in)
    hidden = {0: own}
    for step in (1, 3, 2):
        hidden[step] = along_x(own, step)
    w_both = jnp.concatenate([w_key, w_value], axis=1)
    pair_query = to_pair(w_query)
    w_both = jnp.concatenate([w_query, w_both, pair_query, to_pair(w_both)], axis=1)
    w_back = jnp.concatenate([w_output, to_pair(after(w_output, pair_query))], axis=0)

    angle = positions.astype(jnp.float32)[:, None] * rope_frequencies()[None, :]
    cosine, sine = jnp.cos(angle), jnp.sin(angle)
    cosine = jnp.concatenate([cosine, cosine], axis=1)
    sine = jnp.concatenate([-sine, sine], axis=1)
    kept = jnp.arange(CACHE)[None, None, :] < cache_lengths[:, None, None]
    mask = jnp.where(kept, 0.0, -jnp.inf).astype(jnp.float32)
    mask = jnp.broadcast_to(mask, (mask.shape[0], GROUP, CACHE))
    new_keys = jnp.zeros((ROWS, KVH * DH), jnp.bfloat16)
    new_values = jnp.zeros((ROWS, KVH * DH), jnp.bfloat16)

    terms = []
    came = {}
    for pieces, group in PIECES:
        summed, came = sum_over_plane([hidden[dx] for dx in group], w_both, came)
        packed = [along_x(summed[i], -dx) if dx else summed[i] for i, dx in enumerate(group)]
        chips = jnp.stack([core] + [(x + dx) % SIDE for dx in group]).astype(jnp.int32)
        mixed, new_keys, new_values = attention(
            chips,
            jnp.stack(packed),
            cosine,
            sine,
            mask,
            cache_keys,
            cache_values,
            new_keys,
            new_values,
        )
        rows = [along_x(mixed[i], dx) if dx else mixed[i] for i, dx in enumerate(group)]
        rows = jnp.stack(rows)
        near = {0: rows}
        for step in (2, 1, 3):
            near[step] = along_first(rows, step)
        rows = jnp.stack([near[step] for step in range(SIDE)])
        far = {0: rows}
        for step in (1, 3, 2):
            far[step] = along_second(rows, step)
        for piece in pieces:
            terms += project([far[step] for step in piece], group, w_back)
    attended = add_up(place, terms)
    return (attended.reshape(hidden_in.shape), new_keys, new_values)


def solution(mesh):
    placed = (
        P("gx", "gy"),
        P("gy", "gx"),
        P("gy", "gx"),
        P("gy", "gx"),
        P("gx", "gy"),
        P(("gx", "gy"), None, None),
        P(("gx", "gy"), None, None),
        P(("gx", "gy")),
        P(("gx", "gy")),
    )
    return jax.shard_map(
        on_device,
        mesh=mesh,
        in_specs=placed,
        out_specs=(P("gx", "gy"), P(("gx", "gy"), None), P(("gx", "gy"), None)),
        check_vma=False,
    )
```

```python
import functools
import math

import jax
import jax.numpy as jnp
from jax import lax
from jax.experimental import pallas as pl
from jax.experimental.pallas import tpu as pltpu
from jax.sharding import PartitionSpec as P

HQ = 128
KVH = 8
DH = 128
CACHE = 448
GROUP = HQ // KVH
AXES = ("gx", "gy")
SIDE = 4
ROWS = 8
LIFT = 32.0
PIECES = ((((0, 1, 2, 3),), (1, 3)), (((0, 1, 3), (2,)), (0, 2)))


def rope_frequencies():
    index = jnp.arange(DH // 2, dtype=jnp.float32)
    base = jnp.power(jnp.float32(500000.0), -2.0 * index / DH)
    wavelength = 2.0 * math.pi / base
    smooth = (8192.0 / wavelength - 1.0) / 3.0
    middle = (1.0 - smooth) * base / 8.0 + smooth * base
    return jnp.where(wavelength > 8192.0, base / 8.0, jnp.where(wavelength < 2048.0, base, middle))


def permute(value, move):
    pairs = []
    for x in range(SIDE):
        for c in range(2):
            for z in range(SIDE):
                for y in range(SIDE):
                    tx, tc, tz, ty = move(x, c, z, y)
                    target = ((tx % SIDE) * 2 + tc) * SIDE + tz % SIDE
                    source = (x * 2 + c) * SIDE + z
                    pairs.append((source * SIDE + y, target * SIDE + ty % SIDE))
    return lax.ppermute(value, AXES, pairs)


def to_pair(value):
    return permute(value, lambda x, c, z, y: (x, 1 - c, z, y))


def along_x(value, step):
    return permute(value, lambda x, c, z, y: (x + step, c, z, y))


def along_first(value, step):
    return permute(value, lambda x, c, z, y: (x, c, z + step * c, y + step * (1 - c)))


def along_second(value, step):
    return permute(value, lambda x, c, z, y: (x, c, z + step * (1 - c), y + step * c))


def group_at(place, first, second, sign):
    z, y, core = place[0], place[1], place[2]
    dz = jnp.where(core == 0, second, first)
    dy = jnp.where(core == 0, first, second)
    return lax.rem(z + sign * dz + SIDE, SIDE) * SIDE + lax.rem(y + sign * dy + SIDE, SIDE)


def order_kernel(place, h_ref, out_ref):
    for first in range(SIDE):
        for second in range(SIDE):
            out_ref[first, second] = h_ref[group_at(place, first, second, 1)]


def order_rows(place, hidden):
    width = hidden.shape[1]
    return pl.pallas_call(
        order_kernel,
        out_shape=jax.ShapeDtypeStruct((SIDE, SIDE, ROWS, width), hidden.dtype),
        in_specs=[pl.BlockSpec(memory_space=pltpu.SMEM), pl.BlockSpec(memory_space=pltpu.VMEM)],
        out_specs=pl.BlockSpec(memory_space=pltpu.VMEM),
        cost_estimate=pl.CostEstimate(flops=0, bytes_accessed=2**19, transcendentals=0),
        name="order_rows",
    )(place, hidden.reshape(SIDE * SIDE, ROWS, width))


def total_of(first, others):
    return functools.reduce(
        jnp.add, [first.astype(jnp.float32)] + [item.astype(jnp.float32) for item in others]
    )


def after(value, *others):
    return lax.optimization_barrier((value, *others))[0]


def sum_over_plane(groups, weights, earlier, hold):
    width = weights.shape[1]
    rows = jnp.stack(groups, axis=2)
    rows = rows.reshape(SIDE, SIDE * len(groups) * ROWS, rows.shape[-1])

    terms = {}
    for pair in ((1, 3), (2, 0)):
        value = jnp.concatenate([rows[step] for step in pair], axis=0)
        value = jnp.dot(value, weights, preferred_element_type=jnp.float32)
        value = (value * LIFT).astype(jnp.float16).reshape(2, -1, width)
        terms |= {step: value[i] for i, step in enumerate(pair)}
    came = {}
    for step in (1, 3, 2):
        message = after(terms[step], earlier[step]) if earlier else terms[step]
        came[step] = along_first(message, step)
    kept = total_of(after(terms[0], hold), came.values()).reshape(SIDE, len(groups) * ROWS, width)
    last = [along_second(kept[step].astype(jnp.float16), step) for step in (2, 1, 3)]
    kept = total_of(kept[0], last) * (1.0 / LIFT)
    return kept.astype(jnp.bfloat16).reshape(len(groups), ROWS, width), came, message


def attention_kernel(
    place,
    q_ref,
    cos_ref,
    sin_ref,
    mask_ref,
    k_ref,
    v_ref,
    *refs,
):
    o_ref, nk_ref, nv_ref, queries, results = refs[-5:]
    cosine = cos_ref[...]
    sine = sin_ref[...]
    scale = DH ** (-0.5)
    for pair in range(2):
        base = pair * (GROUP + 2) * DH

        def column(h):
            return q_ref[0, :, base + h * DH : base + (h + 1) * DH]

        def rotated(h):
            u = column(h).astype(jnp.float32)
            return (u * cosine + pltpu.roll(u, DH // 2, 1) * sine).astype(jnp.bfloat16)

        head = pl.ds(pl.multiple_of((place[0] + pair) % 2 * DH, DH), DH)
        for h in range(GROUP):
            queries[pair, pl.ds(h, ROWS, stride=GROUP), :] = rotated(h).astype(jnp.float32)
        key_new = rotated(GROUP)
        value_new = column(GROUP + 1)
        nk_ref[:, head] = key_new
        nv_ref[:, head] = value_new
        key_new = key_new.astype(jnp.float32)
        value_new = value_new.astype(jnp.float32)
        q = queries[pair].reshape(ROWS, GROUP, DH)
        scores = lax.dot_general(
            q.astype(jnp.bfloat16),
            k_ref[:, :, head],
            (((2,), (2,)), ((0,), (0,))),
            preferred_element_type=jnp.float32,
        )
        scores = scores * scale + mask_ref[...]
        score_new = jnp.sum(q * key_new[:, None, :], axis=2, keepdims=True) * scale
        top = jnp.maximum(jnp.max(scores, axis=2, keepdims=True), score_new)
        expo = jnp.exp(scores - top)
        expo_new = jnp.exp(score_new - top)
        share = 1.0 / (jnp.sum(expo, axis=2, keepdims=True) + expo_new)
        weights = (expo * share).astype(jnp.bfloat16)
        weight_new = (expo_new * share).astype(jnp.bfloat16).astype(jnp.float32)
        result = lax.dot_general(
            weights,
            v_ref[:, :, head],
            (((2,), (1,)), ((0,), (0,))),
            preferred_element_type=jnp.float32,
        )
        result = result + weight_new * value_new[:, None, :]
        results[pair] = result.reshape(ROWS * GROUP, DH)
        for h in range(GROUP):
            where = (pair * GROUP + h) * DH
            o_ref[0, :, where : where + DH] = results[
                pair, pl.ds(h, ROWS, stride=GROUP), :
            ].astype(jnp.bfloat16)


def attention(place, packed, cosine, sine, mask, cache_keys, cache_values, written):
    steps, _, width = packed.shape
    chip = KVH // SIDE * DH
    cache = pl.BlockSpec((ROWS, CACHE, chip), lambda r, place: (0, 0, place[1 + r]))
    whole = pl.BlockSpec((ROWS, DH), lambda r, place: (0, 0))
    column = pl.BlockSpec((ROWS, chip), lambda r, place: (0, place[1 + r]))
    new = jax.ShapeDtypeStruct((ROWS, KVH * DH), jnp.bfloat16)
    return pl.pallas_call(
        attention_kernel,
        out_shape=(jax.ShapeDtypeStruct((steps, ROWS, chip * GROUP), jnp.bfloat16), new, new),
        grid_spec=pltpu.PrefetchScalarGridSpec(
            num_scalar_prefetch=1,
            grid=(steps,),
            in_specs=[
                pl.BlockSpec((1, ROWS, width), lambda r, place: (r, 0, 0)),
                whole,
                whole,
                pl.BlockSpec((ROWS, GROUP, CACHE), lambda r, place: (0, 0, 0)),
                cache,
                cache,
            ]
            + [pl.BlockSpec(memory_space=pl.ANY)] * len(written),
            out_specs=(
                pl.BlockSpec((1, ROWS, chip * GROUP), lambda r, place: (r, 0, 0)),
                column,
                column,
            ),
            scratch_shapes=[pltpu.VMEM((2, ROWS * GROUP, DH), jnp.float32)] * 2,
        ),
        input_output_aliases={7: 1, 8: 2} if written else {},
        compiler_params=pltpu.CompilerParams(vmem_limit_bytes=32 * 2**20),
        cost_estimate=pl.CostEstimate(
            flops=4 * ROWS * HQ * CACHE * DH * steps // SIDE,
            bytes_accessed=4 * ROWS * CACHE * KVH * DH * steps // SIDE,
            transcendentals=ROWS * HQ * CACHE * steps // SIDE,
        ),
        name="attention",
    )(place, packed, cosine, sine, mask, cache_keys, cache_values, *written)


def final_kernel(place, *refs):
    terms, out_ref = refs[:-1], refs[-1]
    for second in range(SIDE):
        for first in range(SIDE):
            total = 0.0
            at = 0
            for pieces, group in PIECES:
                for piece in pieces:
                    if second in piece:
                        for term in terms[at : at + len(group)]:
                            total = total + term[piece.index(second), first]
                    at += len(group)
            out_ref[group_at(place, first, second, -1)] = total.astype(jnp.bfloat16)


def add_up(place, terms):
    width = terms[0].shape[-1]
    return pl.pallas_call(
        final_kernel,
        out_shape=jax.ShapeDtypeStruct((SIDE * SIDE, ROWS, width), jnp.bfloat16),
        in_specs=[pl.BlockSpec(memory_space=pltpu.SMEM)]
        + [pl.BlockSpec(memory_space=pltpu.VMEM)] * len(terms),
        out_specs=pl.BlockSpec(memory_space=pltpu.VMEM),
        cost_estimate=pl.CostEstimate(flops=2**19, bytes_accessed=2**21, transcendentals=0),
        name="add_up",
    )(place, *terms)


def project(parts, group, w_output):
    rows = jnp.concatenate([part.reshape(-1, part.shape[-1]) for part in parts], axis=0)
    terms = jnp.dot(rows, w_output, preferred_element_type=jnp.float32)
    terms = terms.reshape(len(parts), SIDE, len(group), ROWS, -1)
    sent = [along_x(terms[:, :, i], -dx) if dx else terms[:, :, i] for i, dx in enumerate(group)]
    return sent, terms


def on_device(
    hidden_in, w_query, w_key, w_value, w_output, cache_keys, cache_values, cache_lengths, positions
):
    gx = lax.axis_index("gx")
    gy = lax.axis_index("gy")
    x, core = gx // 2, gx % 2
    place = jnp.stack([gy // SIDE, gy % SIDE, core]).astype(jnp.int32)

    own = order_rows(place, hidden_in)
    hidden = {0: own}
    for step in (1, 3):
        hidden[step] = along_x(own, step)
    hidden[2] = along_x(after(own, hidden[1], hidden[3]), 2)
    w_both = jnp.concatenate([w_key, w_value], axis=1)
    pair_query = to_pair(w_query)
    w_in = jnp.concatenate([w_query, w_both, pair_query, to_pair(w_both)], axis=1)
    w_back = jnp.concatenate([w_output, to_pair(after(w_output, pair_query))], axis=0)

    angle = positions.astype(jnp.float32)[:, None] * rope_frequencies()[None, :]
    cosine, sine = jnp.cos(angle), jnp.sin(angle)
    cosine = jnp.concatenate([cosine, cosine], axis=1)
    sine = jnp.concatenate([-sine, sine], axis=1)
    kept = jnp.arange(CACHE)[None, None, :] < cache_lengths[:, None, None]
    mask = jnp.where(kept, 0.0, -jnp.inf).astype(jnp.float32)
    mask = jnp.broadcast_to(mask, (mask.shape[0], GROUP, CACHE))
    new = ()

    terms = []
    came, far, ready, local = {}, {}, w_in, None
    for pieces, group in PIECES:
        rows = [after(hidden[dx], ready) for dx in group]
        summed, came, ready = sum_over_plane(rows, w_in, came, w_back)
        packed = [along_x(summed[i], -dx) if dx else summed[i] for i, dx in enumerate(group)]
        chips = jnp.stack([core] + [(x + dx) % SIDE for dx in group]).astype(jnp.int32)
        packed = jnp.stack(packed)
        mixed, *new = attention(chips, packed, cosine, sine, mask, cache_keys, cache_values, new)
        rows = [along_x(mixed[i], dx) if dx else mixed[i] for i, dx in enumerate(group)]
        rows = after(jnp.stack(rows), to_pair(mixed[0, :, :DH]))
        near = {0: rows}
        for step in (2, 1, 3):
            near[step] = along_first(rows, step)
        rows = jnp.stack([near[step] for step in range(SIDE)])
        before, far = far, {0: rows}
        for step in (1, 3, 2):
            message = after(rows, before[step]) if before else rows
            if local is not None and step == 2:
                message = after(message, local)
            far[step] = along_second(message, step)
        earlier = list(terms)
        for piece in pieces:
            parts = [after(far[step], *earlier) for step in piece]
            sent, local = project(parts, group, w_back)
            terms += sent
    attended = add_up(place, terms)
    return (attended.reshape(hidden_in.shape), *new)


def solution(mesh):
    placed = (
        P("gx", "gy"),
        P("gy", "gx"),
        P("gy", "gx"),
        P("gy", "gx"),
        P("gx", "gy"),
        P(("gx", "gy"), None, None),
        P(("gx", "gy"), None, None),
        P(("gx", "gy")),
        P(("gx", "gy")),
    )
    return jax.shard_map(
        on_device,
        mesh=mesh,
        in_specs=placed,
        out_specs=(P("gx", "gy"), P(("gx", "gy"), None), P(("gx", "gy"), None)),
        check_vma=False,
    )
```

```python
import functools
import math

import jax
import jax.numpy as jnp
from jax import lax
from jax.experimental import pallas as pl
from jax.experimental.pallas import tpu as pltpu
from jax.sharding import PartitionSpec as P

HQ = 128
KVH = 8
DH = 128
CACHE = 448
GROUP = HQ // KVH
AXES = ("gx", "gy")
SIDE = 4
ROWS = 8
LIFT = 32.0
PIECES = ((((0, 1, 2, 3),), (1, 3)), (((0, 1, 3), (2,)), (0, 2)))


def rope_frequencies():
    index = jnp.arange(DH // 2, dtype=jnp.float32)
    base = jnp.power(jnp.float32(500000.0), -2.0 * index / DH)
    wavelength = 2.0 * math.pi / base
    smooth = (8192.0 / wavelength - 1.0) / 3.0
    middle = (1.0 - smooth) * base / 8.0 + smooth * base
    return jnp.where(wavelength > 8192.0, base / 8.0, jnp.where(wavelength < 2048.0, base, middle))


def permute(value, move):
    pairs = []
    for x in range(SIDE):
        for c in range(2):
            for z in range(SIDE):
                for y in range(SIDE):
                    tx, tc, tz, ty = move(x, c, z, y)
                    target = ((tx % SIDE) * 2 + tc) * SIDE + tz % SIDE
                    source = (x * 2 + c) * SIDE + z
                    pairs.append((source * SIDE + y, target * SIDE + ty % SIDE))
    return lax.ppermute(value, AXES, pairs)


def to_pair(value):
    return permute(value, lambda x, c, z, y: (x, 1 - c, z, y))


def along_x(value, step):
    return permute(value, lambda x, c, z, y: (x + step, c, z, y))


def along_first(value, step):
    return permute(value, lambda x, c, z, y: (x, c, z + step * c, y + step * (1 - c)))


def along_second(value, step):
    return permute(value, lambda x, c, z, y: (x, c, z + step * (1 - c), y + step * c))


def group_at(place, first, second, sign):
    z, y, core = place[0], place[1], place[2]
    dz = jnp.where(core == 0, second, first)
    dy = jnp.where(core == 0, first, second)
    return lax.rem(z + sign * dz + SIDE, SIDE) * SIDE + lax.rem(y + sign * dy + SIDE, SIDE)


def order_kernel(place, h_ref, out_ref):
    for first in range(SIDE):
        for second in range(SIDE):
            out_ref[first, second] = h_ref[group_at(place, first, second, 1)]


def order_rows(place, hidden):
    width = hidden.shape[1]
    return pl.pallas_call(
        order_kernel,
        out_shape=jax.ShapeDtypeStruct((SIDE, SIDE, ROWS, width), hidden.dtype),
        in_specs=[pl.BlockSpec(memory_space=pltpu.SMEM), pl.BlockSpec(memory_space=pltpu.VMEM)],
        out_specs=pl.BlockSpec(memory_space=pltpu.VMEM),
        cost_estimate=pl.CostEstimate(flops=0, bytes_accessed=2**19, transcendentals=0),
        name="order_rows",
    )(place, hidden.reshape(SIDE * SIDE, ROWS, width))


def total_of(first, others):
    return functools.reduce(
        jnp.add, [first.astype(jnp.float32)] + [item.astype(jnp.float32) for item in others]
    )


def after(value, *others):
    return lax.optimization_barrier((value, *others))[0]


def sum_over_plane(groups, weights, earlier, hold):
    width = weights.shape[1]
    rows = jnp.stack(groups, axis=2)
    rows = rows.reshape(SIDE, SIDE * len(groups) * ROWS, rows.shape[-1])

    terms = {}
    for pair in ((1, 3), (2, 0)):
        value = jnp.concatenate([rows[step] for step in pair], axis=0)
        value = jnp.dot(value, weights, preferred_element_type=jnp.float32)
        value = (value * LIFT).astype(jnp.float16).reshape(2, -1, width)
        terms |= {step: value[i] for i, step in enumerate(pair)}
    came = {}
    for step in (1, 3, 2):
        message = after(terms[step], earlier[step]) if earlier else terms[step]
        came[step] = along_first(message, step)
    kept = total_of(after(terms[0], hold), came.values()).reshape(SIDE, len(groups) * ROWS, width)
    last = [along_second(kept[step].astype(jnp.float16), step) for step in (2, 1, 3)]
    kept = total_of(kept[0], last) * (1.0 / LIFT)
    return kept.astype(jnp.bfloat16).reshape(len(groups), ROWS, width), came, message


def attention_kernel(
    place,
    q_ref,
    cos_ref,
    sin_ref,
    mask_ref,
    k_ref,
    v_ref,
    *refs,
):
    o_ref, nk_ref, nv_ref, queries, results = refs[-5:]
    cosine = cos_ref[...]
    sine = sin_ref[...]
    scale = DH ** (-0.5)
    for pair in range(2):
        base = pair * (GROUP + 2) * DH

        def column(h):
            return q_ref[0, :, base + h * DH : base + (h + 1) * DH]

        def rotated(h):
            u = column(h).astype(jnp.float32)
            return (u * cosine + pltpu.roll(u, DH // 2, 1) * sine).astype(jnp.bfloat16)

        head = pl.ds(pl.multiple_of((place[0] + pair) % 2 * DH, DH), DH)
        for h in range(GROUP):
            queries[pair, pl.ds(h, ROWS, stride=GROUP), :] = rotated(h).astype(jnp.float32)
        key_new = rotated(GROUP)
        value_new = column(GROUP + 1)
        nk_ref[:, head] = key_new
        nv_ref[:, head] = value_new
        key_new = key_new.astype(jnp.float32)
        value_new = value_new.astype(jnp.float32)
        q = queries[pair].reshape(ROWS, GROUP, DH)
        scores = lax.dot_general(
            q.astype(jnp.bfloat16),
            k_ref[:, :, head],
            (((2,), (2,)), ((0,), (0,))),
            preferred_element_type=jnp.float32,
        )
        scores = scores * scale + mask_ref[...]
        score_new = jnp.sum(q * key_new[:, None, :], axis=2, keepdims=True) * scale
        top = jnp.maximum(jnp.max(scores, axis=2, keepdims=True), score_new)
        expo = jnp.exp(scores - top)
        expo_new = jnp.exp(score_new - top)
        share = 1.0 / (jnp.sum(expo, axis=2, keepdims=True) + expo_new)
        weights = (expo * share).astype(jnp.bfloat16)
        weight_new = (expo_new * share).astype(jnp.bfloat16).astype(jnp.float32)
        result = lax.dot_general(
            weights,
            v_ref[:, :, head],
            (((2,), (1,)), ((0,), (0,))),
            preferred_element_type=jnp.float32,
        )
        result = result + weight_new * value_new[:, None, :]
        results[pair] = result.reshape(ROWS * GROUP, DH)
        for h in range(GROUP):
            where = (pair * GROUP + h) * DH
            o_ref[0, :, where : where + DH] = results[
                pair, pl.ds(h, ROWS, stride=GROUP), :
            ].astype(jnp.bfloat16)


def attention(place, packed, cosine, sine, mask, cache_keys, cache_values, written):
    steps, _, width = packed.shape
    chip = KVH // SIDE * DH
    cache = pl.BlockSpec((ROWS, CACHE, chip), lambda r, place: (0, 0, place[1 + r]))
    whole = pl.BlockSpec((ROWS, DH), lambda r, place: (0, 0))
    column = pl.BlockSpec((ROWS, chip), lambda r, place: (0, place[1 + r]))
    new = jax.ShapeDtypeStruct((ROWS, KVH * DH), jnp.bfloat16)
    return pl.pallas_call(
        attention_kernel,
        out_shape=(jax.ShapeDtypeStruct((steps, ROWS, chip * GROUP), jnp.bfloat16), new, new),
        grid_spec=pltpu.PrefetchScalarGridSpec(
            num_scalar_prefetch=1,
            grid=(steps,),
            in_specs=[
                pl.BlockSpec((1, ROWS, width), lambda r, place: (r, 0, 0)),
                whole,
                whole,
                pl.BlockSpec((ROWS, GROUP, CACHE), lambda r, place: (0, 0, 0)),
                cache,
                cache,
            ]
            + [pl.BlockSpec(memory_space=pl.ANY)] * len(written),
            out_specs=(
                pl.BlockSpec((1, ROWS, chip * GROUP), lambda r, place: (r, 0, 0)),
                column,
                column,
            ),
            scratch_shapes=[pltpu.VMEM((2, ROWS * GROUP, DH), jnp.float32)] * 2,
        ),
        input_output_aliases={7: 1, 8: 2} if written else {},
        compiler_params=pltpu.CompilerParams(vmem_limit_bytes=32 * 2**20),
        cost_estimate=pl.CostEstimate(
            flops=4 * ROWS * HQ * CACHE * DH * steps // SIDE,
            bytes_accessed=4 * ROWS * CACHE * KVH * DH * steps // SIDE,
            transcendentals=ROWS * HQ * CACHE * steps // SIDE,
        ),
        name="attention",
    )(place, packed, cosine, sine, mask, cache_keys, cache_values, *written)


def final_kernel(place, *refs):
    terms, out_ref = refs[:-1], refs[-1]
    for second in range(SIDE):
        for first in range(SIDE):
            total = 0.0
            at = 0
            for pieces, group in PIECES:
                for piece in pieces:
                    if second in piece:
                        for term in terms[at : at + len(group)]:
                            total = total + term[piece.index(second), first].astype(jnp.float32)
                    at += len(group)
            out_ref[group_at(place, first, second, -1)] = total.astype(jnp.bfloat16)


def add_up(place, terms):
    width = terms[0].shape[-1]
    return pl.pallas_call(
        final_kernel,
        out_shape=jax.ShapeDtypeStruct((SIDE * SIDE, ROWS, width), jnp.bfloat16),
        in_specs=[pl.BlockSpec(memory_space=pltpu.SMEM)]
        + [pl.BlockSpec(memory_space=pltpu.VMEM)] * len(terms),
        out_specs=pl.BlockSpec(memory_space=pltpu.VMEM),
        cost_estimate=pl.CostEstimate(flops=2**19, bytes_accessed=2**21, transcendentals=0),
        name="add_up",
    )(place, *terms)


def project(parts, group, w_output):
    rows = jnp.concatenate([part.reshape(-1, part.shape[-1]) for part in parts], axis=0)
    terms = jnp.dot(rows, w_output, preferred_element_type=jnp.float32)
    terms = terms.reshape(len(parts), SIDE, len(group), ROWS, -1)
    parts = [terms[:, :, i] for i in range(len(group))]
    sent = [
        along_x(part.astype(jnp.bfloat16), -dx) if dx else part for part, dx in zip(parts, group)
    ]
    return sent, terms


def on_device(
    hidden_in, w_query, w_key, w_value, w_output, cache_keys, cache_values, cache_lengths, positions
):
    gx = lax.axis_index("gx")
    gy = lax.axis_index("gy")
    x, core = gx // 2, gx % 2
    place = jnp.stack([gy // SIDE, gy % SIDE, core]).astype(jnp.int32)

    own = order_rows(place, hidden_in)
    hidden = {0: own}
    for step in (1, 3):
        hidden[step] = along_x(own, step)
    hidden[2] = along_x(after(own, hidden[1], hidden[3]), 2)
    w_both = jnp.concatenate([w_key, w_value], axis=1)
    pair_query = to_pair(w_query)
    w_in = jnp.concatenate([w_query, w_both, pair_query, to_pair(w_both)], axis=1)
    w_back = jnp.concatenate([w_output, to_pair(after(w_output, pair_query))], axis=0)

    angle = positions.astype(jnp.float32)[:, None] * rope_frequencies()[None, :]
    cosine, sine = jnp.cos(angle), jnp.sin(angle)
    cosine = jnp.concatenate([cosine, cosine], axis=1)
    sine = jnp.concatenate([-sine, sine], axis=1)
    kept = jnp.arange(CACHE)[None, None, :] < cache_lengths[:, None, None]
    mask = jnp.where(kept, 0.0, -jnp.inf).astype(jnp.float32)
    mask = jnp.broadcast_to(mask, (mask.shape[0], GROUP, CACHE))
    new = ()

    terms = []
    came, ready, returned = {}, w_in, []
    for _, group in PIECES:
        rows = [after(hidden[dx], ready) for dx in group]
        summed, came, ready = sum_over_plane(rows, w_in, came, w_back)
        packed = [along_x(summed[i], -dx) if dx else summed[i] for i, dx in enumerate(group)]
        chips = jnp.stack([core] + [(x + dx) % SIDE for dx in group]).astype(jnp.int32)
        packed = jnp.stack(packed)
        mixed, *new = attention(chips, packed, cosine, sine, mask, cache_keys, cache_values, new)
        rows = [along_x(mixed[i], dx) if dx else mixed[i] for i, dx in enumerate(group)]
        returned.append(jnp.stack(rows))

    met = to_pair(mixed[0, :, :DH])
    far, local = {}, None
    for (pieces, group), rows in zip(PIECES, returned):
        rows = after(rows, met)
        near = {0: rows}
        for step in (2, 1, 3):
            near[step] = along_first(rows, step)
        rows = jnp.stack([near[step] for step in range(SIDE)])
        before, far = far, {0: rows}
        for step in (1, 3, 2):
            message = after(rows, before[step]) if before else rows
            if local is not None and step == 2:
                message = after(message, local)
            far[step] = along_second(message, step)
        earlier = list(terms)
        for piece in pieces:
            parts = [after(far[step], *earlier) for step in piece]
            sent, local = project(parts, group, w_back)
            terms += sent
    attended = add_up(place, terms)
    return (attended.reshape(hidden_in.shape), *new)


def solution(mesh):
    placed = (
        P("gx", "gy"),
        P("gy", "gx"),
        P("gy", "gx"),
        P("gy", "gx"),
        P("gx", "gy"),
        P(("gx", "gy"), None, None),
        P(("gx", "gy"), None, None),
        P(("gx", "gy")),
        P(("gx", "gy")),
    )
    return jax.shard_map(
        on_device,
        mesh=mesh,
        in_specs=placed,
        out_specs=(P("gx", "gy"), P(("gx", "gy"), None), P(("gx", "gy"), None)),
        check_vma=False,
    )
```

```python
import functools
import math

import jax
import jax.numpy as jnp
from jax import lax
from jax.experimental import pallas as pl
from jax.experimental.pallas import tpu as pltpu
from jax.sharding import PartitionSpec as P

HQ = 128
KVH = 8
DH = 128
CACHE = 448
GROUP = HQ // KVH
AXES = ("gx", "gy")
SIDE = 4
ROWS = 8
LIFT = 32.0
PIECES = ((((0, 1, 2, 3),), (1, 3)), (((0, 1, 3), (2,)), (0, 2)))


def rope_frequencies():
    index = jnp.arange(DH // 2, dtype=jnp.float32)
    base = jnp.power(jnp.float32(500000.0), -2.0 * index / DH)
    wavelength = 2.0 * math.pi / base
    smooth = (8192.0 / wavelength - 1.0) / 3.0
    middle = (1.0 - smooth) * base / 8.0 + smooth * base
    return jnp.where(wavelength > 8192.0, base / 8.0, jnp.where(wavelength < 2048.0, base, middle))


def permute(value, move):
    pairs = []
    for x in range(SIDE):
        for c in range(2):
            for z in range(SIDE):
                for y in range(SIDE):
                    tx, tc, tz, ty = move(x, c, z, y)
                    target = ((tx % SIDE) * 2 + tc) * SIDE + tz % SIDE
                    source = (x * 2 + c) * SIDE + z
                    pairs.append((source * SIDE + y, target * SIDE + ty % SIDE))
    return lax.ppermute(value, AXES, pairs)


def to_pair(value):
    return permute(value, lambda x, c, z, y: (x, 1 - c, z, y))


def along_x(value, step):
    return permute(value, lambda x, c, z, y: (x + step, c, z, y))


def along_first(value, step):
    return permute(value, lambda x, c, z, y: (x, c, z + step * c, y + step * (1 - c)))


def along_second(value, step):
    return permute(value, lambda x, c, z, y: (x, c, z + step * (1 - c), y + step * c))


def group_at(place, first, second, sign):
    z, y, core = place[0], place[1], place[2]
    dz = jnp.where(core == 0, second, first)
    dy = jnp.where(core == 0, first, second)
    return lax.rem(z + sign * dz + SIDE, SIDE) * SIDE + lax.rem(y + sign * dy + SIDE, SIDE)


def order_kernel(place, h_ref, out_ref):
    for first in range(SIDE):
        for second in range(SIDE):
            out_ref[first, second] = h_ref[group_at(place, first, second, 1)]


def order_rows(place, hidden):
    width = hidden.shape[1]
    return pl.pallas_call(
        order_kernel,
        out_shape=jax.ShapeDtypeStruct((SIDE, SIDE, ROWS, width), hidden.dtype),
        in_specs=[pl.BlockSpec(memory_space=pltpu.SMEM), pl.BlockSpec(memory_space=pltpu.VMEM)],
        out_specs=pl.BlockSpec(memory_space=pltpu.VMEM),
        cost_estimate=pl.CostEstimate(flops=0, bytes_accessed=2**19, transcendentals=0),
        name="order_rows",
    )(place, hidden.reshape(SIDE * SIDE, ROWS, width))


def total_of(first, others):
    return functools.reduce(
        jnp.add, [first.astype(jnp.float32)] + [item.astype(jnp.float32) for item in others]
    )


def after(value, *others):
    return lax.optimization_barrier((value, *others))[0]


def sum_over_plane(groups, weights, earlier, hold):
    width = weights.shape[1]
    rows = jnp.stack(groups, axis=2)
    rows = rows.reshape(SIDE, SIDE * len(groups) * ROWS, rows.shape[-1])

    terms = {}
    for pair in ((1, 3), (2, 0)):
        value = jnp.concatenate([rows[step] for step in pair], axis=0)
        value = jnp.dot(value, weights, preferred_element_type=jnp.float32)
        value = (value * LIFT).astype(jnp.float16).reshape(2, -1, width)
        terms |= {step: value[i] for i, step in enumerate(pair)}
    came = {}
    for step in (1, 3, 2):
        message = after(terms[step], earlier[step]) if earlier else terms[step]
        came[step] = along_first(message, step)
    kept = total_of(after(terms[0], hold), came.values()).reshape(SIDE, len(groups) * ROWS, width)
    last = [along_second(kept[step].astype(jnp.float16), step) for step in (2, 1, 3)]
    kept = total_of(kept[0], last) * (1.0 / LIFT)
    return kept.astype(jnp.bfloat16).reshape(len(groups), ROWS, width), came, message


def attention_kernel(
    place,
    q_ref,
    cos_ref,
    sin_ref,
    mask_ref,
    k_ref,
    v_ref,
    *refs,
):
    o_ref, nk_ref, nv_ref, queries, results = refs[-5:]
    cosine = cos_ref[...]
    sine = sin_ref[...]
    scale = DH ** (-0.5)
    for pair in range(2):
        base = pair * (GROUP + 2) * DH

        def column(h):
            return q_ref[0, :, base + h * DH : base + (h + 1) * DH]

        def rotated(h):
            u = column(h).astype(jnp.float32)
            return (u * cosine + pltpu.roll(u, DH // 2, 1) * sine).astype(jnp.bfloat16)

        head = pl.ds(pl.multiple_of((place[0] + pair) % 2 * DH, DH), DH)
        for h in range(GROUP):
            queries[pair, pl.ds(h, ROWS, stride=GROUP), :] = rotated(h).astype(jnp.float32)
        key_new = rotated(GROUP)
        value_new = column(GROUP + 1)
        nk_ref[:, head] = key_new
        nv_ref[:, head] = value_new
        key_new = key_new.astype(jnp.float32)
        value_new = value_new.astype(jnp.float32)
        q = queries[pair].reshape(ROWS, GROUP, DH)
        scores = lax.dot_general(
            q.astype(jnp.bfloat16),
            k_ref[:, :, head],
            (((2,), (2,)), ((0,), (0,))),
            preferred_element_type=jnp.float32,
        )
        scores = scores * scale + mask_ref[...]
        score_new = jnp.sum(q * key_new[:, None, :], axis=2, keepdims=True) * scale
        top = jnp.maximum(jnp.max(scores, axis=2, keepdims=True), score_new)
        expo = jnp.exp(scores - top)
        expo_new = jnp.exp(score_new - top)
        share = 1.0 / (jnp.sum(expo, axis=2, keepdims=True) + expo_new)
        weights = (expo * share).astype(jnp.bfloat16)
        weight_new = (expo_new * share).astype(jnp.bfloat16).astype(jnp.float32)
        result = lax.dot_general(
            weights,
            v_ref[:, :, head],
            (((2,), (1,)), ((0,), (0,))),
            preferred_element_type=jnp.float32,
        )
        result = result + weight_new * value_new[:, None, :]
        results[pair] = result.reshape(ROWS * GROUP, DH)
        for h in range(GROUP):
            where = (pair * GROUP + h) * DH
            o_ref[0, :, where : where + DH] = results[
                pair, pl.ds(h, ROWS, stride=GROUP), :
            ].astype(jnp.bfloat16)


def attention(place, packed, cosine, sine, mask, cache_keys, cache_values, written):
    steps, _, width = packed.shape
    chip = KVH // SIDE * DH
    cache = pl.BlockSpec((ROWS, CACHE, chip), lambda r, place: (0, 0, place[1 + r]))
    whole = pl.BlockSpec((ROWS, DH), lambda r, place: (0, 0))
    column = pl.BlockSpec((ROWS, chip), lambda r, place: (0, place[1 + r]))
    new = jax.ShapeDtypeStruct((ROWS, KVH * DH), jnp.bfloat16)
    return pl.pallas_call(
        attention_kernel,
        out_shape=(jax.ShapeDtypeStruct((steps, ROWS, chip * GROUP), jnp.bfloat16), new, new),
        grid_spec=pltpu.PrefetchScalarGridSpec(
            num_scalar_prefetch=1,
            grid=(steps,),
            in_specs=[
                pl.BlockSpec((1, ROWS, width), lambda r, place: (r, 0, 0)),
                whole,
                whole,
                pl.BlockSpec((ROWS, GROUP, CACHE), lambda r, place: (0, 0, 0)),
                cache,
                cache,
            ]
            + [pl.BlockSpec(memory_space=pl.ANY)] * len(written),
            out_specs=(
                pl.BlockSpec((1, ROWS, chip * GROUP), lambda r, place: (r, 0, 0)),
                column,
                column,
            ),
            scratch_shapes=[pltpu.VMEM((2, ROWS * GROUP, DH), jnp.float32)] * 2,
        ),
        input_output_aliases={7: 1, 8: 2} if written else {},
        compiler_params=pltpu.CompilerParams(vmem_limit_bytes=32 * 2**20),
        cost_estimate=pl.CostEstimate(
            flops=4 * ROWS * HQ * CACHE * DH * steps // SIDE,
            bytes_accessed=4 * ROWS * CACHE * KVH * DH * steps // SIDE,
            transcendentals=ROWS * HQ * CACHE * steps // SIDE,
        ),
        name="attention",
    )(place, packed, cosine, sine, mask, cache_keys, cache_values, *written)


def final_kernel(place, *refs):
    terms, out_ref = refs[:-1], refs[-1]
    for second in range(SIDE):
        for first in range(SIDE):
            total = 0.0
            at = 0
            for pieces, group in PIECES:
                for piece in pieces:
                    if second in piece:
                        for term in terms[at : at + len(group)]:
                            total = total + term[piece.index(second), first].astype(jnp.float32)
                    at += len(group)
            out_ref[group_at(place, first, second, -1)] = total.astype(jnp.bfloat16)


def add_up(place, terms):
    width = terms[0].shape[-1]
    return pl.pallas_call(
        final_kernel,
        out_shape=jax.ShapeDtypeStruct((SIDE * SIDE, ROWS, width), jnp.bfloat16),
        in_specs=[pl.BlockSpec(memory_space=pltpu.SMEM)]
        + [pl.BlockSpec(memory_space=pltpu.VMEM)] * len(terms),
        out_specs=pl.BlockSpec(memory_space=pltpu.VMEM),
        compiler_params=pltpu.CompilerParams(vmem_limit_bytes=6 * 2**20),
        cost_estimate=pl.CostEstimate(flops=2**19, bytes_accessed=2**21, transcendentals=0),
        name="add_up",
    )(place, *terms)


def project(parts, group, w_output):
    rows = jnp.concatenate([part.reshape(-1, part.shape[-1]) for part in parts], axis=0)
    terms = jnp.dot(rows, w_output, preferred_element_type=jnp.float32)
    terms = terms.reshape(len(parts), SIDE, len(group), ROWS, -1)
    parts = [terms[:, :, i] for i in range(len(group))]
    sent = [
        along_x(part.astype(jnp.bfloat16), -dx) if dx else part for part, dx in zip(parts, group)
    ]
    return sent, terms


def on_device(
    hidden_in, w_query, w_key, w_value, w_output, cache_keys, cache_values, cache_lengths, positions
):
    gx = lax.axis_index("gx")
    gy = lax.axis_index("gy")
    x, core = gx // 2, gx % 2
    place = jnp.stack([gy // SIDE, gy % SIDE, core]).astype(jnp.int32)

    own = order_rows(place, hidden_in)
    hidden = {0: own}
    for step in (1, 3):
        hidden[step] = along_x(own, step)
    hidden[2] = along_x(after(own, hidden[1], hidden[3]), 2)
    w_both = jnp.concatenate([w_key, w_value], axis=1)
    pair_query = to_pair(w_query)
    w_in = jnp.concatenate([w_query, w_both, pair_query, to_pair(w_both)], axis=1)
    w_back = jnp.concatenate([w_output, to_pair(after(w_output, pair_query))], axis=0)

    angle = positions.astype(jnp.float32)[:, None] * rope_frequencies()[None, :]
    cosine, sine = jnp.cos(angle), jnp.sin(angle)
    cosine = jnp.concatenate([cosine, cosine], axis=1)
    sine = jnp.concatenate([-sine, sine], axis=1)
    kept = jnp.arange(CACHE)[None, None, :] < cache_lengths[:, None, None]
    mask = jnp.where(kept, 0.0, -jnp.inf).astype(jnp.float32)
    mask = jnp.broadcast_to(mask, (mask.shape[0], GROUP, CACHE))
    new = ()

    terms = []
    came, ready, returned = {}, w_in, []
    for _, group in PIECES:
        rows = [after(hidden[dx], ready) for dx in group]
        summed, came, ready = sum_over_plane(rows, w_in, came, w_back)
        packed = [along_x(summed[i], -dx) if dx else summed[i] for i, dx in enumerate(group)]
        chips = jnp.stack([core] + [(x + dx) % SIDE for dx in group]).astype(jnp.int32)
        packed = jnp.stack(packed)
        mixed, *new = attention(chips, packed, cosine, sine, mask, cache_keys, cache_values, new)
        rows = [along_x(mixed[i], dx) if dx else mixed[i] for i, dx in enumerate(group)]
        returned.append(jnp.stack(rows))

    met = to_pair(mixed[0, :, :DH])
    far, local = {}, None
    for (pieces, group), rows in zip(PIECES, returned):
        rows = after(rows, met)
        near = {0: rows}
        for step in (2, 1, 3):
            near[step] = along_first(rows, step)
        rows = jnp.stack([near[step] for step in range(SIDE)])
        before, far = far, {0: rows}
        for step in (1, 3, 2):
            message = after(rows, before[step]) if before else rows
            if local is not None and step == 2:
                message = after(message, local)
            far[step] = along_second(message, step)
        earlier = list(terms)
        for piece in pieces:
            parts = [after(far[step], *earlier) for step in piece]
            sent, local = project(parts, group, w_back)
            terms += sent
    attended = add_up(place, terms)
    return (attended.reshape(hidden_in.shape), *new)


def solution(mesh):
    placed = (
        P("gx", "gy"),
        P("gy", "gx"),
        P("gy", "gx"),
        P("gy", "gx"),
        P("gx", "gy"),
        P(("gx", "gy"), None, None),
        P(("gx", "gy"), None, None),
        P(("gx", "gy")),
        P(("gx", "gy")),
    )
    return jax.shard_map(
        on_device,
        mesh=mesh,
        in_specs=placed,
        out_specs=(P("gx", "gy"), P(("gx", "gy"), None), P(("gx", "gy"), None)),
        check_vma=False,
    )
```
